128 devices in a mesh: space: 16 (over y, z), freq: 8 (over x, core).
Axes of the slice: x: 4, y: 4, z: 4, core: 2. Of those that a mesh axis runs over, the one named last changes fastest.
Arguments:
- source: float32 [2, 16, 128, 32768], P(None, None, 'space', 'freq'), may hold values from -6 to 6
- angles: float32 [4, 16, 128, 32768], P(None, None, 'space', 'freq'), may hold values from -3.140625 to 3.140625
- cheb_tables: float32 [4, 4, 2, 2, 16, 16], replicated, may hold values from -1 to 1
- switch_kernel: float32 [2, 16, 16], replicated, may hold values from -1 to 1
- box_class: int32 [4, 128], replicated, may hold values from 0 to 3
Outputs:
- spectrum: float32 [2, 16, 128, 32768], P(None, None, 'space', 'freq')
The draws below stay inside these ranges and needn't reach their ends.
All inputs are finite; a program needn't handle non-finite values.
Results may differ from the reference program's by a relative error of at most 0.0003.
Values sent between devices are 32-bit elements; how exact they have to be, the bound alone decides.
No kernel may reach another device: no remote copies, remote signals or barrier semaphores. Data moves between devices by JAX's collectives and lax.ppermute only.
A program may use at most 256 MiB of HBM per device.

```python
import jax
import jax.numpy as jnp
from jax import lax

R = 16
LEVELS = 4
NCLASS = 4
S_DEV = 8
F_DEV = 4096
NS = 128
NF = 32768
N_SPACE = 16
N_FREQ = 8


def place_ends(array, rng, least, high):
    index_at = [jax.random.randint(jax.random.fold_in(rng, axis), (), 0, length) for axis, length in enumerate(array.shape)]
    widest = array.shape.index(max(array.shape))
    beside = index_at[:widest] + [(index_at[widest] + 1) % array.shape[widest]] + index_at[widest + 1:]
    return array.at[tuple(index_at)].set(least).at[tuple(beside)].set(high)


def levels(key, dims, shards, low, largest):
    gain, own = 1.0, jax.random.fold_in(key, 6)
    for position, shards_of in shards:
        steps = jnp.exp(jax.random.uniform(jax.random.fold_in(own, position), (shards_of,), jnp.float32, low / len(shards), largest / len(shards)))
        gain = gain * jnp.repeat(steps, dims[position] // shards_of).reshape([-1 if axis == position else 1 for axis in range(len(dims))])
    return gain


def scatter_about(own_key, dims, width, reach, shards=(), kind=jnp.bfloat16):
    values = width * jax.random.normal(own_key, dims, jnp.float32)
    if shards:
        values = values * levels(own_key, dims, shards, -0.22, 0.18)
    return jnp.clip(values, -reach, reach).astype(kind)


def setup_inputs(seed: int = 0) -> dict:
    seeds = jax.random.split(jax.random.key(seed), 6)
    source = scatter_about(seeds[0], (2, R, NS, NF), 1.0, 6.0, ((2, 16), (3, 8)), jnp.float32)
    angles = jnp.clip(jax.random.uniform(seeds[1], (LEVELS, R, NS, NF), jnp.float32, -3.140625, 3.140625), -3.140625, 3.140625)
    cheb_tables = scatter_about(seeds[2], (LEVELS, NCLASS, 2, 2, R, R), (2 * R) ** -0.5, 1.0, (), jnp.float32)
    switch_kernel = scatter_about(seeds[3], (2, R, R), (2 * R) ** -0.5, 1.0, (), jnp.float32)
    box_class = place_ends(jax.random.randint(seeds[4], (LEVELS, NS), 0, NCLASS), jax.random.fold_in(seeds[4], 1), 0, NCLASS - 1).astype(jnp.int32)
    return {"source": source, "angles": angles, "cheb_tables": cheb_tables, "switch_kernel": switch_kernel, "box_class": box_class}


def rotate(values, phases):
    cosine = jnp.cos(phases)
    sine_part = jnp.sin(phases)
    return jnp.stack([cosine * values[0] - sine_part * values[1], sine_part * values[0] + cosine * values[1]])


def apply_boxes(weight, values):
    return jnp.einsum("pts,cspf->ctpf", weight, values, precision=lax.Precision.HIGHEST)


def apply_kernel(kernel, values):
    full_shape = values.shape
    flattened = values.reshape(2, full_shape[1], -1)
    real_part = jnp.dot(kernel[0], flattened[0], precision=lax.Precision.HIGHEST) - jnp.dot(kernel[1], flattened[1], precision=lax.Precision.HIGHEST)
    imag_part = jnp.dot(kernel[0], flattened[1], precision=lax.Precision.HIGHEST) + jnp.dot(kernel[1], flattened[0], precision=lax.Precision.HIGHEST)
    return jnp.stack([real_part, imag_part]).reshape(full_shape)


def reference(source, angles, cheb_tables, switch_kernel, box_class):
    current = source
    bit_count = N_SPACE.bit_length() - 1
    boxes = jnp.arange(NS).astype(jnp.int32)
    for level_number in range(LEVELS):
        stride = S_DEV * 2 ** (level_number % bit_count)
        halves = (boxes // stride) % 2
        rotated = rotate(current, angles[level_number])
        partner = rotated[:, :, boxes ^ stride, :]
        onehot = (box_class[level_number][:, None] == jnp.arange(NCLASS)[None, :]).astype(jnp.float32)
        tables = jnp.einsum("pk,khjts->phjts", onehot, cheb_tables[level_number], precision=lax.Precision.HIGHEST)
        mine = jnp.where(halves[:, None, None, None] == 1, tables[:, 1], tables[:, 0])
        w_self = jnp.where(halves[:, None, None] == 1, mine[:, 1], mine[:, 0])
        w_other = jnp.where(halves[:, None, None] == 1, mine[:, 0], mine[:, 1])
        current = apply_boxes(w_self, rotated) + apply_boxes(w_other, partner)
        if level_number == LEVELS // 2 - 1:
            current = apply_kernel(switch_kernel, current)
            blocks = current.reshape(2, R, NS, N_FREQ, N_FREQ, F_DEV // N_FREQ)
            current = blocks.transpose(0, 1, 2, 4, 3, 5).reshape(2, R, NS, NF)
    return current
```

```python
import functools

import jax
import jax.numpy as jnp
from jax import lax
from jax.experimental import pallas as pl
from jax.experimental.pallas import tpu as pltpu
from jax.sharding import PartitionSpec as P

NCLASS = 4
PTS = 16
BOX = 8
FL = 4096
CH = 2
Q = 4
HIGHEST = lax.Precision.HIGHEST
SIN = (1.0, -0.04166664555668831, 0.0005208156653679907, -3.095163492616848e-06, 1.0176427700514523e-08)
COS = (0.9999999403953552, -0.1249997615814209, 0.002603973727673292, -2.1646354070981033e-05, 9.044205739883182e-08)
VMEM = 56 * 1024 * 1024


def poly(coefs, u):
    r = coefs[-1]
    for c in coefs[-2::-1]:
        r = r * u + c
    return r


def turn(re, im, a):
    u = a * a
    s2 = a * poly(SIN, u)
    sine = s2 * poly(COS, u)
    cosine = 1.0 - 0.5 * (s2 * s2)
    return cosine * re - sine * im, sine * re + cosine * im


def split3(x):
    hi = x.astype(jnp.bfloat16)
    lo = (x - hi.astype(jnp.float32)).astype(jnp.bfloat16)
    return jnp.concatenate([hi, lo, hi], axis=0)


def mm(w, x):
    return jnp.dot(w, split3(x), preferred_element_type=jnp.float32)


def first_kernel(k, zr, s0, s1, s2, s3, a0, a1, a2, a3, o0, o1, o2, o3):
    for s, a, o in ((s0, a0, o0), (s1, a1, o1), (s2, a2, o2), (s3, a3, o3)):
        for j in range(Q):
            rows = pl.ds(Q * k + j, PTS, stride=BOX)
            re, im = turn(s[0, rows, :], s[1, rows, :], a[0, rows, :])
            here = slice(PTS * j, PTS * (j + 1))
            o[0, here, :] = re
            o[1, here, :] = im
            o[2, here, :] = a[1, rows, :]


def first(k, z, source, angles):
    rows = PTS * BOX
    src = [pl.BlockSpec((2, rows, 128), lambda d, zr, e=e: (0, 0, d * Q + (zr[0] ^ e))) for e in range(Q)]
    ang = [pl.BlockSpec((2, rows, 128), lambda d, zr, e=e: (0, 0, d * Q + (zr[0] ^ e))) for e in range(Q)]
    return pl.pallas_call(
        functools.partial(first_kernel, k),
        grid_spec=pltpu.PrefetchScalarGridSpec(
            num_scalar_prefetch=1,
            grid=(8,),
            in_specs=src + ang,
            out_specs=[pl.BlockSpec((3, Q * PTS, 128), lambda d, zr: (0, 0, d))] * Q,
        ),
        out_shape=[jax.ShapeDtypeStruct((3, Q * PTS, 1024), jnp.float32)] * Q,
        compiler_params=pltpu.CompilerParams(vmem_limit_bytes=VMEM),
        cost_estimate=pl.CostEstimate(flops=20_000_000, bytes_accessed=11_000_000, transcendentals=0),
        name="first",
    )(z, *[source] * Q, *[angles] * Q)


def share_kernel(yr, a0, a1, a2, a3, o0, o1, o2, o3):
    for e, o in enumerate((o0, o1, o2, o3)):
        for k in range(CH):
            for l in range(2):
                for i, a in enumerate((a0, a1, a2, a3)):
                    o[k, l, :, 128 * i : 128 * i + 128] = a[l, pl.ds(Q * k + (yr[0] ^ e), PTS, stride=BOX), :]


def share(y, angles):
    return pl.pallas_call(
        share_kernel,
        grid_spec=pltpu.PrefetchScalarGridSpec(
            num_scalar_prefetch=1,
            grid=(8,),
            in_specs=[pl.BlockSpec((2, PTS * BOX, 128), lambda d, yr, i=i: (1, 0, 4 * d + i)) for i in range(4)],
            out_specs=[pl.BlockSpec((CH, 2, PTS, 512), lambda d, yr: (0, 0, 0, d))] * Q,
        ),
        out_shape=[jax.ShapeDtypeStruct((CH, 2, PTS, FL), jnp.float32)] * Q,
        compiler_params=pltpu.CompilerParams(vmem_limit_bytes=VMEM),
        cost_estimate=pl.CostEstimate(flops=1_000_000, bytes_accessed=8_400_000, transcendentals=0),
        name="share",
    )(y, *[angles] * 4)


def early_kernel(zr, r0, r1, r2, r3, w0, w1, o):
    r = (r0, r1, r2, r3)
    z = zr[0]
    x = [[None] * Q for _ in range(Q)]
    for q in range(2):
        for g in range(2):
            part = []
            for c in range(2):
                rows = jnp.concatenate([r[2 * q + i][c, 32 * g : 32 * g + 32, :] for i in range(2)], axis=0)
                part.append(mm(w0[q, g], rows))
            for i in range(2):
                e = 2 * q + i
                here = slice(32 * i, 32 * i + 32)
                re, im = turn(part[0][here], part[1][here], r[e][2, 32 * g : 32 * g + 32, :])
                for n in range(2):
                    x[e][2 * g + n] = (re[PTS * n : PTS * n + PTS], im[PTS * n : PTS * n + PTS])
    for j in range(Q):
        for m in range(2):
            rows = jnp.concatenate([*x[m][j], *x[m + 2][j]], axis=0)
            out = mm(w1[j, m], rows)
            for i in range(2):
                for c in range(2):
                    piece = out[32 * i + PTS * c : 32 * i + PTS * c + PTS]
                    for b in range(2):
                        o[j, z ^ (m + 2 * i), b, c] = piece[:, 128 * b : 128 * b + 128]


def early(z, parts, w0, w1):
    return pl.pallas_call(
        early_kernel,
        grid_spec=pltpu.PrefetchScalarGridSpec(
            num_scalar_prefetch=1,
            grid=(4,),
            in_specs=[pl.BlockSpec((3, Q * PTS, 256), lambda d, zr: (0, 0, d))] * Q
            + [
                pl.BlockSpec((2, 2, 64, 192), lambda d, zr: (0, 0, 0, 0)),
                pl.BlockSpec((Q, 2, 64, 192), lambda d, zr: (0, 0, 0, 0)),
            ],
            out_specs=pl.BlockSpec((Q, Q, 2, 2, PTS, 128), lambda d, zr: (0, 0, d, 0, 0, 0)),
        ),
        out_shape=jax.ShapeDtypeStruct((Q, Q, 8, 2, PTS, 128), jnp.float32),
        compiler_params=pltpu.CompilerParams(vmem_limit_bytes=VMEM),
        cost_estimate=pl.CostEstimate(flops=400_000_000, bytes_accessed=5_000_000, transcendentals=0),
        name="early",
    )(z, *parts, w0, w1)


def late_kernel(yr, x, a0, a1, a2, a3, w2, w3, o0, o1, o2, o3):
    y = yr[0]
    angles = [jnp.concatenate([a[0, l] for a in (a0, a1, a2, a3)], axis=0) for l in range(2)]
    pair = []
    for c in range(2):
        pair.append(
            jnp.concatenate(
                [jnp.concatenate([x[y ^ e, t, 0, c] for t in range(Q)], axis=1) for e in range(Q)], axis=0
            )
        )
    for l, w in enumerate((w2, w3)):
        pair = [mm(w[...], v) for v in turn(*pair, angles[l])]
    for e, o in enumerate((o0, o1, o2, o3)):
        for c in range(2):
            o[c] = pair[c][PTS * e : PTS * e + PTS]


def late(k, y, x, angles, w2, w3):
    return pl.pallas_call(
        late_kernel,
        grid_spec=pltpu.PrefetchScalarGridSpec(
            num_scalar_prefetch=1,
            grid=(8,),
            in_specs=[pl.BlockSpec((Q, Q, 1, 2, PTS, 128), lambda d, yr: (0, 0, d, 0, 0, 0))]
            + [pl.BlockSpec((1, 2, PTS, 512), lambda d, yr: (k, 0, 0, d))] * Q
            + [pl.BlockSpec((64, 192), lambda d, yr: (0, 0))] * 2,
            out_specs=[pl.BlockSpec((2, PTS, 512), lambda d, yr: (0, 0, d))] * Q,
        ),
        out_shape=[jax.ShapeDtypeStruct((2, PTS, FL), jnp.float32)] * Q,
        compiler_params=pltpu.CompilerParams(vmem_limit_bytes=VMEM),
        cost_estimate=pl.CostEstimate(flops=400_000_000, bytes_accessed=5_000_000, transcendentals=0),
        name="late",
    )(y, x, *angles, w2, w3)


def last_kernel(yr, *refs):
    o, room = refs[-2:]
    for c in range(2):
        for i in range(4):
            lanes = slice(128 * i, 128 * i + 128)
            for k in range(CH):
                for e in range(Q):
                    room[c, i, pl.ds(Q * k + (yr[0] ^ e), PTS, stride=BOX), :] = refs[Q * k + e][c, :, lanes]
            o[c, :, lanes] = room[c, i]


def last(y, parts):
    return pl.pallas_call(
        last_kernel,
        grid_spec=pltpu.PrefetchScalarGridSpec(
            num_scalar_prefetch=1,
            grid=(8,),
            in_specs=[pl.BlockSpec((2, PTS, 512), lambda d, yr: (0, 0, d))] * (CH * Q),
            out_specs=pl.BlockSpec((2, PTS * BOX, 512), lambda d, yr: (0, 0, d)),
            scratch_shapes=[pltpu.VMEM((2, 4, PTS * BOX, 128), jnp.float32)],
        ),
        out_shape=jax.ShapeDtypeStruct((2, PTS * BOX, FL), jnp.float32),
        compiler_params=pltpu.CompilerParams(vmem_limit_bytes=VMEM),
        cost_estimate=pl.CostEstimate(flops=1_000_000, bytes_accessed=8_400_000, transcendentals=0),
        name="last",
    )(y, *parts)


def pick(onehot, options):
    shape = onehot.shape + options.shape[1:]
    mask = onehot.reshape(onehot.shape + (1,) * (options.ndim - 1))
    return jnp.sum(jnp.where(mask, jnp.broadcast_to(options, shape), 0.0), axis=onehot.ndim - 1)


def halves(tables, classes, half):
    chosen = pick(classes[..., None] == jnp.arange(NCLASS), tables)
    upper = (half == 1)[:, None, None, None]
    own, other = chosen[:, :, 0, 0], chosen[:, :, 0, 1]
    own = jnp.where(upper, chosen[:, :, 1, 1], own)
    other = jnp.where(upper, chosen[:, :, 1, 0], other)
    return own, other


def two_parts(w):
    hi = lax.reduce_precision(w, 8, 7)
    lo = w - hi
    return jnp.concatenate([hi, hi, lo], axis=-1).astype(jnp.bfloat16)


def weights(cheb_tables, switch_kernel, box_class, y, z):
    near = jnp.arange(Q)
    byplace = box_class.reshape(4, Q, Q, BOX)
    mine_y = lax.dynamic_index_in_dim(byplace, y, 1, False)
    mine_z = lax.dynamic_index_in_dim(byplace, z, 2, False)
    by_z = pick((z ^ near)[:, None] == near, mine_y.transpose(1, 0, 2)).astype(jnp.int32)
    by_y = pick((y ^ near)[:, None] == near, mine_z.transpose(1, 0, 2)).astype(jnp.int32)
    eye = jnp.eye(2, dtype=jnp.float32)
    k0, k1 = switch_kernel[0], switch_kernel[1]
    kc = jnp.stack([jnp.stack([k0, -k1]), jnp.stack([k1, k0])])

    own, other = halves(cheb_tables[0], by_z[:, 0], (z ^ near) & 1)
    own, other = (v.reshape(2, 2, CH, 2, 2, PTS, PTS) for v in (own, other))
    w0 = jnp.einsum("qikgnts,ij,nm->kqgintjms", own, eye, eye, precision=HIGHEST)
    w0 += jnp.einsum("qikgnts,ij,nm->kqgintjms", other, 1 - eye, eye, precision=HIGHEST)
    w0 = w0.reshape(CH, 2, 2, 64, 64)

    own, other = halves(cheb_tables[1], by_z[:, 1], ((z ^ near) >> 1) & 1)
    own, other = (
        jnp.einsum("cdtu,pus->pctds", kc, v.reshape(32, PTS, PTS), precision=HIGHEST).reshape(
            2, 2, CH, Q, 2, PTS, 2, PTS
        )
        for v in (own, other)
    )
    w1 = jnp.einsum("imkjctds,ih->kjmicthds", own, eye, precision=HIGHEST)
    w1 += jnp.einsum("imkjctds,ih->kjmicthds", other, 1 - eye, precision=HIGHEST)
    w1 = w1.reshape(CH, Q, 2, 64, 64)

    late_w = []
    for l in (2, 3):
        own, other = halves(cheb_tables[l], by_y[:, l], ((y ^ near) >> (l - 2)) & 1)
        at = (y == near)[None, None]
        own, other = (
            jnp.sum(jnp.where(at[..., None, None], v.reshape(Q, CH, Q, PTS, PTS), 0.0), axis=2) for v in (own, other)
        )
        same = jnp.eye(Q, dtype=jnp.float32)
        swap = (near[:, None] ^ (l - 1) == near).astype(jnp.float32)
        w = jnp.einsum("ekts,eh->keths", own, same, precision=HIGHEST)
        w += jnp.einsum("ekts,eh->keths", other, swap, precision=HIGHEST)
        late_w.append(two_parts(w.reshape(CH, 64, 64)))
    return two_parts(w0), two_parts(w1), late_w[0], late_w[1]


def exchange(parts, stride):
    count = lax.axis_size("space")
    return [parts[0]] + [
        lax.ppermute(parts[e], "space", [(i, i ^ (stride * e)) for i in range(count)]) for e in range(1, Q)
    ]


def on_device(source, angles, cheb_tables, switch_kernel, box_class):
    place = lax.axis_index("space")
    y, z = place // Q, place % Q
    yr, zr = y.reshape(1).astype(jnp.int32), z.reshape(1).astype(jnp.int32)
    source = source.reshape(2, PTS * BOX, FL)
    angles = angles.reshape(4, PTS * BOX, FL)

    sent_a = first(0, zr, source, angles)
    sent_a, (source, angles) = lax.optimization_barrier((sent_a, (source, angles)))
    here_a = exchange(sent_a, 1)
    late_angles = exchange(share(yr, angles), Q)
    sent_b = first(1, zr, source, angles)
    sent_b, cheb_tables, switch_kernel, box_class = lax.optimization_barrier(
        (sent_b, cheb_tables, switch_kernel, box_class)
    )
    w0, w1, w2, w3 = weights(cheb_tables, switch_kernel, box_class, y, z)
    here_a, sent_b = lax.optimization_barrier((here_a, sent_b))
    here_b = exchange(sent_b, 1)

    result = []
    for k, here in enumerate((here_a, here_b)):
        mixed = early(zr, here, w0[k], w1[k])
        moved = lax.all_to_all(mixed.reshape(128, 2, PTS, 128), ("space", "freq"), 0, 0, tiled=True)
        done = late(k, yr, moved.reshape(Q, Q, 8, 2, PTS, 128), late_angles, w2[k], w3[k])
        result += exchange(done, Q)
    return last(yr, result).reshape(2, PTS, BOX, FL)


def solution(mesh):
    in_specs = (P(None, None, "space", "freq"), P(None, None, "space", "freq"), P(), P(), P())
    out_specs = P(None, None, "space", "freq")
    return jax.shard_map(
        on_device, mesh=mesh, in_specs=in_specs, out_specs=out_specs, check_vma=False
    )
```

```python
import functools

import jax
import jax.numpy as jnp
from jax import lax
from jax.experimental import pallas as pl
from jax.experimental.pallas import tpu as pltpu
from jax.sharding import PartitionSpec as P

NCLASS = 4
PTS = 16
BOX = 8
FL = 4096
CH = 2
Q = 4
HIGHEST = lax.Precision.HIGHEST
SIN = (1.0, -0.04166664555668831, 0.0005208156653679907, -3.095163492616848e-06, 1.0176427700514523e-08)
COS = (0.9999999403953552, -0.1249997615814209, 0.002603973727673292, -2.1646354070981033e-05, 9.044205739883182e-08)
VMEM = 56 * 1024 * 1024
COST = pl.CostEstimate(flops=1000, bytes_accessed=1000, transcendentals=0)


def poly(coefs, u):
    r = coefs[-1]
    for c in coefs[-2::-1]:
        r = r * u + c
    return r


def turn(re, im, a):
    u = a * a
    s2 = a * poly(SIN, u)
    sine = s2 * poly(COS, u)
    cosine = 1.0 - 0.5 * (s2 * s2)
    return cosine * re - sine * im, sine * re + cosine * im


def split3(x):
    hi = x.astype(jnp.bfloat16)
    lo = (x - hi.astype(jnp.float32)).astype(jnp.bfloat16)
    return jnp.concatenate([hi, lo, hi], axis=0)


def mm(w, x):
    return jnp.dot(w, split3(x), preferred_element_type=jnp.float32)


def by_box(v):
    return jnp.swapaxes(v.reshape(PTS, BOX, v.shape[-1]), 0, 1)


def first_kernel(n, zr, *refs):
    src, ang, outs, room = refs[:n], refs[n : 2 * n], refs[2 * n : 2 * n + Q], refs[-1]
    for d in range(n):
        re, im = turn(src[d][0], src[d][1], ang[d][0])
        for c, v in enumerate((re, im, ang[d][1])):
            room[c] = by_box(v)
        for e, o in enumerate(outs):
            for c in range(3):
                for i in range(2):
                    o[c, PTS * i : PTS * i + PTS, 256 * d : 256 * d + 256] = room[c, 2 * (zr[0] ^ e) + i]


def first(k, z, source, angles, n=2):
    def spec(d):
        return pl.BlockSpec((2, PTS * BOX, 256), lambda g, zr: (0, 0, 2 * (n * g + d) + k))

    return pl.pallas_call(
        functools.partial(first_kernel, n),
        grid_spec=pltpu.PrefetchScalarGridSpec(
            num_scalar_prefetch=1,
            grid=(8 // n,),
            in_specs=[spec(d) for d in range(n)] * 2,
            out_specs=[pl.BlockSpec((3, 2 * PTS, 256 * n), lambda g, zr: (0, 0, g))] * Q,
            scratch_shapes=[pltpu.VMEM((3, BOX, PTS, 256), jnp.float32)],
        ),
        out_shape=[jax.ShapeDtypeStruct((3, 2 * PTS, 2048), jnp.float32)] * Q,
        compiler_params=pltpu.CompilerParams(vmem_limit_bytes=VMEM),
        cost_estimate=COST,
        name="first",
    )(z, *[source] * n, *[angles] * n)


def share_kernel(yr, a, o0, o1, o2, o3, room):
    for l in range(2):
        for d in range(4):
            for t in range(Q):
                here = slice(512 * d + 128 * t, 512 * d + 128 * t + 128)
                v = by_box(a[l, :, here]).reshape(Q, 2, PTS, 128)
                for n in range(2):
                    room[t // 2, 2 * (t % 2) + n] = v[:, n].reshape(Q * PTS, 128)
            for e, o in enumerate((o0, o1, o2, o3)):
                for k in range(CH):
                    o[k, l, :, 128 * d : 128 * d + 128] = room[k, yr[0] ^ e]


def share(y, angles):
    return pl.pallas_call(
        share_kernel,
        grid_spec=pltpu.PrefetchScalarGridSpec(
            num_scalar_prefetch=1,
            grid=(2,),
            in_specs=[pl.BlockSpec((2, PTS * BOX, 2048), lambda d, yr: (1, 0, d))],
            out_specs=[pl.BlockSpec((CH, 2, Q * PTS, 512), lambda d, yr: (0, 0, 0, d))] * Q,
            scratch_shapes=[pltpu.VMEM((CH, Q, Q * PTS, 128), jnp.float32)],
        ),
        out_shape=[jax.ShapeDtypeStruct((CH, 2, Q * PTS, 1024), jnp.float32)] * Q,
        compiler_params=pltpu.CompilerParams(vmem_limit_bytes=VMEM),
        cost_estimate=COST,
        name="share",
    )(y, angles)


def early_kernel(zr, r0, r1, r2, r3, w0, w1, o):
    r = (r0, r1, r2, r3)
    x = []
    for q in range(2):
        part = []
        for c in range(2):
            rows = jnp.concatenate([r[2 * q + i][c] for i in range(2)], axis=0)
            part.append(mm(w0[0, q], rows))
        angle = jnp.concatenate([r[2 * q + i][2] for i in range(2)], axis=0)
        x.append(turn(*part, angle))
    for n in range(2):
        for m in range(2):
            here = slice(32 * m + PTS * n, 32 * m + PTS * n + PTS)
            rows = jnp.concatenate([x[i][c][here] for i in range(2) for c in range(2)], axis=0)
            out = mm(w1[0, n, m], rows)
            for i in range(2):
                for c in range(2):
                    piece = out[32 * i + PTS * c : 32 * i + PTS * c + PTS]
                    for t in range(piece.shape[1] // 128):
                        o[2 * (t % 2) + n, zr[0] ^ (m + 2 * i), t // 2, c] = piece[:, 128 * t : 128 * t + 128]


def early(k, z, parts, w0, w1, steps=4):
    lanes, n = 2048 // steps, 8 // steps
    return pl.pallas_call(
        early_kernel,
        grid_spec=pltpu.PrefetchScalarGridSpec(
            num_scalar_prefetch=1,
            grid=(steps,),
            in_specs=[pl.BlockSpec((3, 2 * PTS, lanes), lambda d, zr: (0, 0, d))] * Q
            + [
                pl.BlockSpec((1, 2, 64, 192), lambda d, zr: (0, 0, 0, 0)),
                pl.BlockSpec((1, 2, 2, 64, 192), lambda d, zr: (0, 0, 0, 0, 0)),
            ],
            out_specs=pl.BlockSpec((Q, Q, n, 2, PTS, 128), lambda d, zr: (0, 0, d, 0, 0, 0)),
        ),
        out_shape=jax.ShapeDtypeStruct((Q, Q, 8, 2, PTS, 128), jnp.float32),
        compiler_params=pltpu.CompilerParams(vmem_limit_bytes=VMEM),
        cost_estimate=COST,
        name="early",
    )(z, *parts, w0, w1)


def late_kernel(yr, x, a0, a1, a2, a3, w2, w3, o0, o1, o2, o3):
    y = yr[0]
    count = x.shape[2]
    for t in range(Q):
        here = slice(PTS * t, PTS * t + PTS)
        angles = [jnp.concatenate([a[0, l, here] for a in (a0, a1, a2, a3)], axis=0) for l in range(2)]
        pair = []
        for c in range(2):
            pair.append(
                jnp.concatenate(
                    [jnp.concatenate([x[y ^ e, t, d, c] for d in range(count)], axis=1) for e in range(Q)], axis=0
                )
            )
        for l, w in enumerate((w2, w3)):
            pair = [mm(w[t], v) for v in turn(*pair, angles[l])]
        for e, o in enumerate((o0, o1, o2, o3)):
            for c in range(2):
                o[c, here] = pair[c][PTS * e : PTS * e + PTS]


def late(k, y, x, angles, w2, w3, steps=4):
    n = 8 // steps
    return pl.pallas_call(
        late_kernel,
        grid_spec=pltpu.PrefetchScalarGridSpec(
            num_scalar_prefetch=1,
            grid=(steps,),
            in_specs=[pl.BlockSpec((Q, Q, n, 2, PTS, 128), lambda d, yr: (0, 0, d, 0, 0, 0))]
            + [pl.BlockSpec((1, 2, Q * PTS, 128 * n), lambda d, yr: (k, 0, 0, d))] * Q
            + [pl.BlockSpec((Q, 64, 192), lambda d, yr: (0, 0, 0))] * 2,
            out_specs=[pl.BlockSpec((2, Q * PTS, 128 * n), lambda d, yr: (0, 0, d))] * Q,
        ),
        out_shape=[jax.ShapeDtypeStruct((2, Q * PTS, 1024), jnp.float32)] * Q,
        compiler_params=pltpu.CompilerParams(vmem_limit_bytes=VMEM),
        cost_estimate=COST,
        name="late",
    )(y, x, *angles, w2, w3)


def last_kernel(k, yr, *refs):
    ins, (o, room, ready, sems) = refs[:Q], refs[-4:]
    copies = []
    for d in range(8):
        here = slice(128 * d, 128 * d + 128)
        for c in range(2):
            for e in range(Q):
                at = yr[0] ^ e
                for t in range(Q):
                    room[at // 2, c, 2 * t + at % 2] = ins[e][c, PTS * t : PTS * t + PTS, here]
        for c in range(2):
            for b in range(2):
                v = jnp.swapaxes(room[b, c], 0, 1).reshape(PTS * BOX, 128)
                ready[c, :, 256 * d + 128 * b : 256 * d + 128 * b + 128] = v
        copies.append(
            pltpu.make_async_copy(
                ready.at[:, :, pl.ds(256 * d, 256)], o.at[:, :, pl.ds(512 * d + 256 * k, 256)], sems.at[d]
            )
        )
        copies[-1].start()
    for copy in copies:
        copy.wait()


def last(k, y, parts, before):
    extra = [] if before is None else [before]
    return pl.pallas_call(
        functools.partial(last_kernel, k),
        grid_spec=pltpu.PrefetchScalarGridSpec(
            num_scalar_prefetch=1,
            grid=(1,),
            in_specs=[pl.BlockSpec((2, Q * PTS, 1024), lambda d, yr: (0, 0, 0))] * Q
            + [pl.BlockSpec(memory_space=pl.ANY)] * len(extra),
            out_specs=pl.BlockSpec(memory_space=pl.ANY),
            scratch_shapes=[
                pltpu.VMEM((2, 2, BOX, PTS, 128), jnp.float32),
                pltpu.VMEM((2, PTS * BOX, 2048), jnp.float32),
                pltpu.SemaphoreType.DMA((8,)),
            ],
        ),
        out_shape=jax.ShapeDtypeStruct((2, PTS * BOX, FL), jnp.float32),
        input_output_aliases={Q + 1: 0} if extra else {},
        compiler_params=pltpu.CompilerParams(vmem_limit_bytes=VMEM),
        cost_estimate=COST,
        name="last",
    )(y, *parts, *extra)


def pick(onehot, options):
    shape = onehot.shape + options.shape[1:]
    mask = onehot.reshape(onehot.shape + (1,) * (options.ndim - 1))
    return jnp.sum(jnp.where(mask, jnp.broadcast_to(options, shape), 0.0), axis=onehot.ndim - 1)


def halves(tables, classes, half):
    chosen = pick(classes[..., None] == jnp.arange(NCLASS), tables)
    upper = (half == 1)[:, None, None, None]
    own, other = chosen[:, :, 0, 0], chosen[:, :, 0, 1]
    own = jnp.where(upper, chosen[:, :, 1, 1], own)
    other = jnp.where(upper, chosen[:, :, 1, 0], other)
    return own, other


def two_parts(w):
    hi = lax.reduce_precision(w, 8, 7)
    lo = w - hi
    return jnp.concatenate([hi, hi, lo], axis=-1).astype(jnp.bfloat16)


def weights(cheb_tables, switch_kernel, box_class, y, z):
    near = jnp.arange(Q)
    byplace = box_class.reshape(4, Q, Q, BOX)
    mine_y = lax.dynamic_index_in_dim(byplace, y, 1, False)
    mine_z = lax.dynamic_index_in_dim(byplace, z, 2, False)
    mine_y = lax.dynamic_slice_in_dim(mine_y, 2 * z, 2, 2)
    mine_z = lax.dynamic_index_in_dim(mine_z.reshape(4, Q, Q, 2), y % 2, 3, False)
    by_z = pick((z ^ near)[:, None] == near, mine_y.transpose(1, 0, 2)).astype(jnp.int32)
    by_y = pick((y ^ near)[:, None] == near, mine_z.transpose(1, 0, 2)).astype(jnp.int32)
    eye = jnp.eye(2, dtype=jnp.float32)
    k0, k1 = switch_kernel[0], switch_kernel[1]
    kc = jnp.stack([jnp.stack([k0, -k1]), jnp.stack([k1, k0])])

    own, other = halves(cheb_tables[0], by_z[:, 0], (z ^ near) & 1)
    own, other = (v.reshape(2, 2, 2, PTS, PTS) for v in (own, other))
    w0 = jnp.einsum("qints,ij,nm->qintjms", own, eye, eye, precision=HIGHEST)
    w0 += jnp.einsum("qints,ij,nm->qintjms", other, 1 - eye, eye, precision=HIGHEST)
    w0 = w0.reshape(1, 2, 64, 64)

    own, other = halves(cheb_tables[1], by_z[:, 1], ((z ^ near) >> 1) & 1)
    own, other = (
        jnp.einsum("cdtu,pus->pctds", kc, v.reshape(8, PTS, PTS), precision=HIGHEST).reshape(2, 2, 2, 2, PTS, 2, PTS)
        for v in (own, other)
    )
    w1 = jnp.einsum("imnctds,ih->nmicthds", own, eye, precision=HIGHEST)
    w1 += jnp.einsum("imnctds,ih->nmicthds", other, 1 - eye, precision=HIGHEST)
    w1 = w1.reshape(1, 2, 2, 64, 64)

    late_w = []
    for l in (2, 3):
        own, other = halves(cheb_tables[l], by_y[:, l], ((y ^ near) >> (l - 2)) & 1)
        same = jnp.eye(Q, dtype=jnp.float32)
        swap = (near[:, None] ^ (l - 1) == near).astype(jnp.float32)
        w = jnp.einsum("ekts,eh->keths", own, same, precision=HIGHEST)
        w += jnp.einsum("ekts,eh->keths", other, swap, precision=HIGHEST)
        late_w.append(two_parts(w.reshape(Q, 64, 64)))
    return two_parts(w0), two_parts(w1), late_w[0], late_w[1]


def exchange(parts, stride):
    count = lax.axis_size("space")
    return [parts[0]] + [
        lax.ppermute(parts[e], "space", [(i, i ^ (stride * e)) for i in range(count)]) for e in range(1, Q)
    ]


def on_device(source, angles, cheb_tables, switch_kernel, box_class):
    place = lax.axis_index("space")
    y, z = place // Q, place % Q
    yr, zr = y.reshape(1).astype(jnp.int32), z.reshape(1).astype(jnp.int32)
    source = source.reshape(2, PTS * BOX, FL)
    angles = angles.reshape(4, PTS * BOX, FL)

    sent_a = first(0, zr, source, angles)
    sent_a, source, angles = lax.optimization_barrier((sent_a, source, angles))
    here_a = exchange(sent_a, 1)
    late_angles = exchange(share(yr, angles), Q)
    sent_b = first(1, zr, source, angles)
    sent_b, cheb_tables, switch_kernel, box_class = lax.optimization_barrier(
        (sent_b, cheb_tables, switch_kernel, box_class)
    )
    w0, w1, w2, w3 = weights(cheb_tables, switch_kernel, box_class, y, z)
    here_a, sent_b = lax.optimization_barrier((here_a, sent_b))
    here_b = exchange(sent_b, 1)

    result = None
    for k, here in enumerate((here_a, here_b)):
        if k == 1:
            here, done = lax.optimization_barrier((here, done))
        mixed = early(k, zr, here, w0, w1)
        moved = lax.all_to_all(mixed.reshape(128, 2, PTS, 128), ("space", "freq"), 0, 0, tiled=True)
        done = late(k, yr, moved.reshape(Q, Q, 8, 2, PTS, 128), late_angles, w2, w3)
        result = last(k, yr, exchange(done, Q), result)
    return result.reshape(2, PTS, BOX, FL)


def solution(mesh):
    in_specs = (P(None, None, "space", "freq"), P(None, None, "space", "freq"), P(), P(), P())
    out_specs = P(None, None, "space", "freq")
    return jax.shard_map(
        on_device, mesh=mesh, in_specs=in_specs, out_specs=out_specs, check_vma=False
    )
```

```python
import functools

import jax
import jax.numpy as jnp
from jax import lax
from jax.experimental import pallas as pl
from jax.experimental.pallas import tpu as pltpu
from jax.sharding import PartitionSpec as P

NCLASS = 4
PTS = 16
BOX = 8
FL = 4096
Q = 4
HIGHEST = lax.Precision.HIGHEST
SIN = (1.0, -0.04166664555668831, 0.0005208156653679907, -3.095163492616848e-06, 1.0176427700514523e-08)
COS = (0.9999999403953552, -0.1249997615814209, 0.002603973727673292, -2.1646354070981033e-05, 9.044205739883182e-08)
VMEM = 56 * 1024 * 1024


def cost(flops=1000):
    return pl.CostEstimate(flops=flops, bytes_accessed=1000, transcendentals=0)


def poly(coefs, u):
    r = coefs[-1]
    for c in coefs[-2::-1]:
        r = r * u + c
    return r


def turn(re, im, a):
    u = a * a
    s2 = a * poly(SIN, u)
    sine = s2 * poly(COS, u)
    cosine = 1.0 - 0.5 * (s2 * s2)
    return cosine * re - sine * im, sine * re + cosine * im


def split3(x):
    hi = x.astype(jnp.bfloat16)
    lo = (x - hi.astype(jnp.float32)).astype(jnp.bfloat16)
    return jnp.concatenate([hi, lo, hi], axis=0)


def mm(w, x):
    return jnp.dot(w, split3(x), preferred_element_type=jnp.float32)


def by_box(v):
    return jnp.swapaxes(v.reshape(PTS, BOX, v.shape[-1]), 0, 1)


def swap_halves(a, b):
    low = lax.broadcasted_iota(jnp.int32, a.shape, a.ndim - 1) < 64
    return (
        jnp.where(low, a, pltpu.roll(b, 64, a.ndim - 1)),
        jnp.where(low, pltpu.roll(a, 64, a.ndim - 1), b),
    )


def first_kernel(n, zr, *refs):
    src, ang, outs, room = refs[:n], refs[n : 2 * n], refs[2 * n : 2 * n + Q], refs[-1]
    lanes = room.shape[-1]
    for d in range(n):
        re, im = turn(src[d][0], src[d][1], ang[d][0])
        for c, v in enumerate((re, im, ang[d][1])):
            room[c] = by_box(v)
        for e, o in enumerate(outs):
            for c in range(3):
                for i in range(2):
                    o[c, PTS * i : PTS * i + PTS, lanes * d : lanes * d + lanes] = room[c, 2 * ((zr[0] + e) % Q) + i]


def first(chunk, z, source, angles):
    tile, count = chunk
    lanes, n = 128 * count, 4

    def spec(d):
        return pl.BlockSpec((2, PTS * BOX, lanes), lambda g, zr: (0, 0, (n * g + d) * (4 // count) + tile // count))

    return pl.pallas_call(
        functools.partial(first_kernel, n),
        grid_spec=pltpu.PrefetchScalarGridSpec(
            num_scalar_prefetch=1,
            grid=(8 // n,),
            in_specs=[spec(d) for d in range(n)] * 2,
            out_specs=[pl.BlockSpec((3, 2 * PTS, lanes * n), lambda g, zr: (0, 0, g))] * Q,
            scratch_shapes=[pltpu.VMEM((3, BOX, PTS, lanes), jnp.float32)],
        ),
        out_shape=[jax.ShapeDtypeStruct((3, 2 * PTS, lanes * 8), jnp.float32)] * Q,
        compiler_params=pltpu.CompilerParams(vmem_limit_bytes=VMEM),
        cost_estimate=cost(),
        name="first",
    )(z, *[source] * n, *[angles] * n)


def share_kernel(yr, a, o0, o1, o2, o3, room):
    for l in range(2):
        for g in range(2):
            for t in range(Q):
                pair = [
                    by_box(a[l, :, 512 * d + 128 * t : 512 * d + 128 * t + 128]).reshape(Q, 2, PTS, 128)
                    for d in (2 * g, 2 * g + 1)
                ]
                for n in range(2):
                    for h, v in enumerate(swap_halves(pair[0][:, n], pair[1][:, n])):
                        room[2 * n + h] = v.reshape(Q * PTS, 128)
                for e, o in enumerate((o0, o1, o2, o3)):
                    o[t, l, :, 128 * g : 128 * g + 128] = room[(yr[0] + e) % Q]


def share(y, angles):
    return pl.pallas_call(
        share_kernel,
        grid_spec=pltpu.PrefetchScalarGridSpec(
            num_scalar_prefetch=1,
            grid=(2,),
            in_specs=[pl.BlockSpec((2, PTS * BOX, 2048), lambda d, yr: (1, 0, d))],
            out_specs=[pl.BlockSpec((4, 2, Q * PTS, 256), lambda d, yr: (0, 0, 0, d))] * Q,
            scratch_shapes=[pltpu.VMEM((Q, Q * PTS, 128), jnp.float32)],
        ),
        out_shape=[jax.ShapeDtypeStruct((4, 2, Q * PTS, 512), jnp.float32)] * Q,
        compiler_params=pltpu.CompilerParams(vmem_limit_bytes=VMEM),
        cost_estimate=cost(),
        name="share",
    )(y, angles)


def early_kernel(zr, r0, r1, r2, r3, w0, w1, o, r):
    for e, v in enumerate((r0, r1, r2, r3)):
        r[(zr[0] + Q - e) % Q] = v[...]
    count = o.shape[3]
    x = []
    for q in range(2):
        part = []
        for c in range(2):
            rows = jnp.concatenate([r[2 * q + i, c] for i in range(2)], axis=0)
            part.append(mm(w0[q], rows))
        angle = jnp.concatenate([r[2 * q + i, 2] for i in range(2)], axis=0)
        x.append(turn(*part, angle))
    for n in range(2):
        for m in range(2):
            here = slice(32 * m + PTS * n, 32 * m + PTS * n + PTS)
            rows = jnp.concatenate([x[i][c][here] for i in range(2) for c in range(2)], axis=0)
            out = mm(w1[n, m], rows)
            for i in range(2):
                both = [out[32 * i + PTS * c : 32 * i + PTS * c + PTS] for c in range(2)]
                for t in range(both[0].shape[1] // 128):
                    pieces = swap_halves(*[v[:, 128 * t : 128 * t + 128] for v in both])
                    for h in range(2):
                        o[2 * n + h, m + 2 * i, t // count, t % count] = pieces[h]


def early(chunk, z, parts, w0, w1, flops, steps=2):
    count = chunk[1]
    n = 8 // steps
    return pl.pallas_call(
        early_kernel,
        grid_spec=pltpu.PrefetchScalarGridSpec(
            num_scalar_prefetch=1,
            grid=(steps,),
            in_specs=[pl.BlockSpec((3, 2 * PTS, 128 * count * n), lambda d, zr: (0, 0, d))] * Q
            + [
                pl.BlockSpec((2, 64, 192), lambda d, zr: (0, 0, 0)),
                pl.BlockSpec((2, 2, 64, 192), lambda d, zr: (0, 0, 0, 0)),
            ],
            out_specs=pl.BlockSpec((Q, Q, n, count, PTS, 128), lambda d, zr: (0, 0, d, 0, 0, 0)),
            scratch_shapes=[pltpu.VMEM((Q, 3, 2 * PTS, 128 * count * n), jnp.float32)],
        ),
        out_shape=jax.ShapeDtypeStruct((Q, Q, 8, count, PTS, 128), jnp.float32),
        compiler_params=pltpu.CompilerParams(vmem_limit_bytes=VMEM),
        cost_estimate=cost(flops),
        name="early",
    )(z, *parts, w0, w1)


def late_kernel(yr, x, a0, a1, a2, a3, w2, w3, o0, o1, o2, o3, turns, done):
    y = yr[0]
    pairs, count = x.shape[2] // 2, x.shape[3]
    for e, a in enumerate((a0, a1, a2, a3)):
        turns[(y + Q - e) % Q] = a[...]
    for j in range(count):
        for t in range(Q):
            here = slice(PTS * t, PTS * t + PTS)
            angles = [jnp.concatenate([turns[e, j, l, here] for e in range(Q)], axis=0) for l in range(2)]
            split = [[swap_halves(x[e, t, 2 * g, j], x[e, t, 2 * g + 1, j]) for g in range(pairs)] for e in range(Q)]
            pair = [
                jnp.concatenate([jnp.concatenate([v[c] for v in row], axis=1) for row in split], axis=0)
                for c in range(2)
            ]
            for l, w in enumerate((w2, w3)):
                pair = [mm(w[t], v) for v in turn(*pair, angles[l])]
            for e in range(Q):
                for c in range(2):
                    done[e, j, c, here] = pair[c][PTS * e : PTS * e + PTS]
    for e, o in enumerate((o0, o1, o2, o3)):
        o[...] = done[(y + e) % Q]


def late(chunk, y, x, angles, w2, w3, flops, steps=2):
    tile, count = chunk
    n = 8 // steps
    return pl.pallas_call(
        late_kernel,
        grid_spec=pltpu.PrefetchScalarGridSpec(
            num_scalar_prefetch=1,
            grid=(steps,),
            in_specs=[pl.BlockSpec((Q, Q, n, count, PTS, 128), lambda d, yr: (0, 0, d, 0, 0, 0))]
            + [pl.BlockSpec((count, 2, Q * PTS, 64 * n), lambda d, yr: (tile // count, 0, 0, d))] * Q
            + [pl.BlockSpec((Q, 64, 192), lambda d, yr: (0, 0, 0))] * 2,
            out_specs=[pl.BlockSpec((count, 2, Q * PTS, 64 * n), lambda d, yr: (0, 0, 0, d))] * Q,
            scratch_shapes=[pltpu.VMEM((Q, count, 2, Q * PTS, 64 * n), jnp.float32)] * 2,
        ),
        out_shape=[jax.ShapeDtypeStruct((count, 2, Q * PTS, 512), jnp.float32)] * Q,
        compiler_params=pltpu.CompilerParams(vmem_limit_bytes=VMEM),
        cost_estimate=cost(flops),
        name="late",
    )(y, x, *angles, w2, w3)


def last_kernel(chunk, yr, *refs):
    tile, count = chunk
    ins, (o, room, ready, sems) = refs[:Q], refs[-4:]
    copies = []
    for g in range(4):
        here = slice(128 * g, 128 * g + 128)
        for j in range(count):
            for c in range(2):
                for e in range(Q):
                    at = (yr[0] + Q - e) % Q
                    for t in range(Q):
                        room[at % 2, 2 * t + at // 2] = ins[e][j, c, PTS * t : PTS * t + PTS, here]
                for i, v in enumerate(swap_halves(room[0], room[1])):
                    lanes = 128 * (count * (2 * g + i) + j)
                    ready[c, :, lanes : lanes + 128] = jnp.swapaxes(v, 0, 1).reshape(PTS * BOX, 128)
        for d in (2 * g, 2 * g + 1):
            copies.append(
                pltpu.make_async_copy(
                    ready.at[:, :, pl.ds(128 * count * d, 128 * count)],
                    o.at[:, :, pl.ds(512 * d + 128 * tile, 128 * count)],
                    sems.at[d],
                )
            )
            copies[-1].start()
    for copy in copies:
        copy.wait()


def last(chunk, y, parts, before):
    extra = [] if before is None else [before]
    count = chunk[1]
    return pl.pallas_call(
        functools.partial(last_kernel, chunk),
        grid_spec=pltpu.PrefetchScalarGridSpec(
            num_scalar_prefetch=1,
            grid=(1,),
            in_specs=[pl.BlockSpec((count, 2, Q * PTS, 512), lambda d, yr: (0, 0, 0, 0))] * Q
            + [pl.BlockSpec(memory_space=pl.ANY)] * len(extra),
            out_specs=pl.BlockSpec(memory_space=pl.ANY),
            scratch_shapes=[
                pltpu.VMEM((2, BOX, PTS, 128), jnp.float32),
                pltpu.VMEM((2, PTS * BOX, 1024 * count), jnp.float32),
                pltpu.SemaphoreType.DMA((8,)),
            ],
        ),
        out_shape=jax.ShapeDtypeStruct((2, PTS * BOX, FL), jnp.float32),
        input_output_aliases={Q + 1: 0} if extra else {},
        compiler_params=pltpu.CompilerParams(vmem_limit_bytes=VMEM),
        cost_estimate=cost(),
        name="last",
    )(y, *parts, *extra)


def pick(onehot, options):
    shape = onehot.shape + options.shape[1:]
    mask = onehot.reshape(onehot.shape + (1,) * (options.ndim - 1))
    return jnp.sum(jnp.where(mask, jnp.broadcast_to(options, shape), 0.0), axis=onehot.ndim - 1)


def halves(tables, classes, half):
    chosen = pick(classes[..., None] == jnp.arange(NCLASS), tables)
    upper = (half == 1)[:, None, None, None]
    own, other = chosen[:, :, 0, 0], chosen[:, :, 0, 1]
    own = jnp.where(upper, chosen[:, :, 1, 1], own)
    other = jnp.where(upper, chosen[:, :, 1, 0], other)
    return own, other


def two_parts(w):
    hi = lax.reduce_precision(w, 8, 7)
    lo = w - hi
    return jnp.concatenate([hi, hi, lo], axis=-1).astype(jnp.bfloat16)


def weights(cheb_tables, switch_kernel, box_class, y, z):
    near = jnp.arange(Q)
    byplace = box_class.reshape(4, Q, Q, BOX)
    mine_y = lax.dynamic_index_in_dim(byplace, y, 1, False)
    mine_z = lax.dynamic_index_in_dim(byplace, z, 2, False)
    mine_y = lax.dynamic_slice_in_dim(mine_y, 2 * z, 2, 2)
    mine_z = lax.dynamic_index_in_dim(mine_z.reshape(4, Q, Q, 2), y // 2, 3, False)
    by_z, by_y = mine_y.transpose(1, 0, 2), mine_z.transpose(1, 0, 2)
    eye = jnp.eye(2, dtype=jnp.float32)
    k0, k1 = switch_kernel[0], switch_kernel[1]
    kc = jnp.stack([jnp.stack([k0, -k1]), jnp.stack([k1, k0])])

    own, other = halves(cheb_tables[0], by_z[:, 0], near & 1)
    own, other = (v.reshape(2, 2, 2, PTS, PTS) for v in (own, other))
    w0 = jnp.einsum("qints,ij,nm->qintjms", own, eye, eye, precision=HIGHEST)
    w0 += jnp.einsum("qints,ij,nm->qintjms", other, 1 - eye, eye, precision=HIGHEST)
    w0 = w0.reshape(2, 64, 64)

    own, other = halves(cheb_tables[1], by_z[:, 1], (near >> 1) & 1)
    own, other = (
        jnp.einsum("cdtu,pus->pctds", kc, v.reshape(8, PTS, PTS), precision=HIGHEST).reshape(2, 2, 2, 2, PTS, 2, PTS)
        for v in (own, other)
    )
    w1 = jnp.einsum("imnctds,ih->nmicthds", own, eye, precision=HIGHEST)
    w1 += jnp.einsum("imnctds,ih->nmicthds", other, 1 - eye, precision=HIGHEST)
    w1 = w1.reshape(2, 2, 64, 64)

    late_w = []
    for l in (2, 3):
        own, other = halves(cheb_tables[l], by_y[:, l], (near >> (l - 2)) & 1)
        same = jnp.eye(Q, dtype=jnp.float32)
        swap = (near[:, None] ^ (l - 1) == near).astype(jnp.float32)
        w = jnp.einsum("ekts,eh->keths", own, same, precision=HIGHEST)
        w += jnp.einsum("ekts,eh->keths", other, swap, precision=HIGHEST)
        late_w.append(two_parts(w.reshape(Q, 64, 64)))
    return two_parts(w0), two_parts(w1), late_w[0], late_w[1]


def swapped(part, e, stride):
    count = lax.axis_size("space")

    def target(i):
        at = i // stride % Q
        return i + ((at + e) % Q - at) * stride

    return lax.ppermute(part, "space", [(i, target(i)) for i in range(count)])


def exchange(parts, stride):
    return [parts[0]] + [swapped(parts[e], e, stride) for e in range(1, Q)]


CHUNKS = ((0, 2), (2, 1), (3, 1))
LONG = 40_000_000_000


def on_device(source, angles, cheb_tables, switch_kernel, box_class):
    place = lax.axis_index("space")
    y, z = place // Q, place % Q
    yr, zr = y.reshape(1).astype(jnp.int32), z.reshape(1).astype(jnp.int32)
    source = source.reshape(2, PTS * BOX, FL)
    angles = angles.reshape(4, PTS * BOX, FL)
    tie = lax.optimization_barrier
    count = len(CHUNKS)

    sent, here, mixed, moved, back = [None] * count, [None] * count, [None] * count, [None] * count, [None] * count
    ready = first(CHUNKS[0], zr, source, angles)
    ready, source, angles = tie((ready, source, angles))
    here[0] = exchange(ready, 1)
    turns = share(yr, angles)
    turns, source, angles = tie((turns, source, angles))
    turns = list(turns)
    turns[1], turns[3] = swapped(turns[1], 1, Q), swapped(turns[3], 3, Q)
    for k in range(1, count):
        sent[k] = first(CHUNKS[k], zr, source, angles)
    sent[1:], cheb_tables, switch_kernel, box_class = tie((sent[1:], cheb_tables, switch_kernel, box_class))
    w0, w1, w2, w3 = weights(cheb_tables, switch_kernel, box_class, y, z)
    here[0], sent[1:], w0, w1, w2, w3 = tie((here[0], sent[1:], w0, w1, w2, w3))

    def do_late(k):
        if k:
            if k + 1 < len(CHUNKS):
                back[k - 1], moved[k] = tie((back[k - 1], moved[k]))
            else:
                back[k - 1][1], moved[k] = tie((back[k - 1][1], moved[k]))
        done = late(CHUNKS[k], yr, moved[k], turns, w2, w3, (8_000_000_000, 7_000_000_000, 1000)[k])
        back[k] = exchange(done, Q)

    for k, chunk in enumerate(CHUNKS):
        if k + 1 < count:
            here[k], sent[k + 1] = tie((here[k], sent[k + 1]))
            here[k + 1] = exchange(sent[k + 1], 1)
        if k == 1:
            here[k], turns[2] = tie((here[k], turns[2]))
        mixed[k] = early(chunk, zr, here[k], w0, w1, (1000, LONG, 3_000_000_000)[k])
        if k:
            moved[k - 1], mixed[k] = tie((moved[k - 1], mixed[k]))
        if k == 0:
            turns[1], turns[2], turns[3] = tie((turns[1], turns[2], turns[3]))
            turns[2] = swapped(turns[2], 2, Q)
        all_parts = lax.all_to_all(mixed[k].reshape(128, chunk[1], PTS, 128), ("space", "freq"), 0, 0, tiled=True)
        moved[k] = all_parts.reshape(Q, Q, 8, chunk[1], PTS, 128)
        if k:
            do_late(k - 1)
            if k + 1 < count:
                back[k - 1][0], here[k + 1] = tie((back[k - 1][0], here[k + 1]))
    do_late(count - 1)
    result = None
    for k, chunk in enumerate(CHUNKS):
        if k + 1 < count:
            back[k], back[k + 1][0] = tie((back[k], back[k + 1][0]))
        result = last(chunk, yr, back[k], result)
    return result.reshape(2, PTS, BOX, FL)


def solution(mesh):
    in_specs = (P(None, None, "space", "freq"), P(None, None, "space", "freq"), P(), P(), P())
    out_specs = P(None, None, "space", "freq")
    return jax.shard_map(
        on_device, mesh=mesh, in_specs=in_specs, out_specs=out_specs, check_vma=False
    )
```

```python
import functools

import jax
import jax.numpy as jnp
from jax import lax
from jax.experimental import pallas as pl
from jax.experimental.pallas import tpu as pltpu
from jax.sharding import PartitionSpec as P

NCLASS = 4
PTS = 16
BOX = 8
FL = 4096
Q = 4
HIGHEST = lax.Precision.HIGHEST
SIN = (1.0, -0.04166664555668831, 0.0005208156653679907, -3.095163492616848e-06, 1.0176427700514523e-08)
COS = (0.9999999403953552, -0.1249997615814209, 0.002603973727673292, -2.1646354070981033e-05, 9.044205739883182e-08)
VMEM = 56 * 1024 * 1024


def cost(flops=1000):
    return pl.CostEstimate(flops=flops, bytes_accessed=1000, transcendentals=0)


def poly(coefs, u):
    r = coefs[-1]
    for c in coefs[-2::-1]:
        r = r * u + c
    return r


def turn(re, im, a):
    u = a * a
    s2 = a * poly(SIN, u)
    sine = s2 * poly(COS, u)
    cosine = 1.0 - 0.5 * (s2 * s2)
    return cosine * re - sine * im, sine * re + cosine * im


def split3(x):
    hi = x.astype(jnp.bfloat16)
    lo = (x - hi.astype(jnp.float32)).astype(jnp.bfloat16)
    return jnp.concatenate([hi, lo, hi], axis=0)


def mm(w, x):
    return jnp.dot(w, split3(x), preferred_element_type=jnp.float32)


def by_box(v):
    return jnp.swapaxes(v.reshape(PTS, BOX, v.shape[-1]), 0, 1)


def swap_halves(a, b):
    low = lax.broadcasted_iota(jnp.int32, a.shape, a.ndim - 1) < 64
    return (
        jnp.where(low, a, pltpu.roll(b, 64, a.ndim - 1)),
        jnp.where(low, pltpu.roll(a, 64, a.ndim - 1), b),
    )


def first_kernel(n, zr, *refs):
    src, ang, outs, room = refs[:n], refs[n : 2 * n], refs[2 * n : 2 * n + Q], refs[-1]
    lanes = room.shape[-1]
    for d in range(n):
        re, im = turn(src[d][0], src[d][1], ang[d][0])
        for c, v in enumerate((re, im, ang[d][1])):
            room[c] = by_box(v)
        for e, o in enumerate(outs):
            for c in range(3):
                for i in range(2):
                    o[c, PTS * i : PTS * i + PTS, lanes * d : lanes * d + lanes] = room[c, 2 * ((zr[0] + e) % Q) + i]


def first(chunk, z, source, angles):
    tile, count = chunk
    lanes, n = 128 * count, 4

    def spec(d):
        return pl.BlockSpec((2, PTS * BOX, lanes), lambda g, zr: (0, 0, (n * g + d) * (4 // count) + tile // count))

    return pl.pallas_call(
        functools.partial(first_kernel, n),
        grid_spec=pltpu.PrefetchScalarGridSpec(
            num_scalar_prefetch=1,
            grid=(8 // n,),
            in_specs=[spec(d) for d in range(n)] * 2,
            out_specs=[pl.BlockSpec((3, 2 * PTS, lanes * n), lambda g, zr: (0, 0, g))] * Q,
            scratch_shapes=[pltpu.VMEM((3, BOX, PTS, lanes), jnp.float32)],
        ),
        out_shape=[jax.ShapeDtypeStruct((3, 2 * PTS, lanes * 8), jnp.float32)] * Q,
        compiler_params=pltpu.CompilerParams(vmem_limit_bytes=VMEM),
        cost_estimate=cost(),
        name="first",
    )(z, *[source] * n, *[angles] * n)


def share_kernel(yr, a, o0, o1, o2, o3, room):
    for l in range(2):
        for g in range(2):
            for t in range(Q):
                pair = [
                    by_box(a[l, :, 512 * d + 128 * t : 512 * d + 128 * t + 128]).reshape(Q, 2, PTS, 128)
                    for d in (2 * g, 2 * g + 1)
                ]
                for n in range(2):
                    for h, v in enumerate(swap_halves(pair[0][:, n], pair[1][:, n])):
                        room[2 * n + h] = v.reshape(Q * PTS, 128)
                for e, o in enumerate((o0, o1, o2, o3)):
                    o[t, l, :, 128 * g : 128 * g + 128] = room[(yr[0] + e) % Q]


def share(y, angles):
    return pl.pallas_call(
        share_kernel,
        grid_spec=pltpu.PrefetchScalarGridSpec(
            num_scalar_prefetch=1,
            grid=(2,),
            in_specs=[pl.BlockSpec((2, PTS * BOX, 2048), lambda d, yr: (1, 0, d))],
            out_specs=[pl.BlockSpec((4, 2, Q * PTS, 256), lambda d, yr: (0, 0, 0, d))] * Q,
            scratch_shapes=[pltpu.VMEM((Q, Q * PTS, 128), jnp.float32)],
        ),
        out_shape=[jax.ShapeDtypeStruct((4, 2, Q * PTS, 512), jnp.float32)] * Q,
        compiler_params=pltpu.CompilerParams(vmem_limit_bytes=VMEM),
        cost_estimate=cost(),
        name="share",
    )(y, angles)


def early_kernel(zr, r0, r1, r2, r3, w0, w1, o, r):
    for e, v in enumerate((r0, r1, r2, r3)):
        r[(zr[0] + Q - e) % Q] = v[...]
    count = o.shape[3]
    x = []
    for q in range(2):
        part = []
        for c in range(2):
            rows = jnp.concatenate([r[2 * q + i, c] for i in range(2)], axis=0)
            part.append(mm(w0[q], rows))
        angle = jnp.concatenate([r[2 * q + i, 2] for i in range(2)], axis=0)
        x.append(turn(*part, angle))
    for n in range(2):
        for m in range(2):
            here = slice(32 * m + PTS * n, 32 * m + PTS * n + PTS)
            rows = jnp.concatenate([x[i][c][here] for i in range(2) for c in range(2)], axis=0)
            out = mm(w1[n, m], rows)
            for i in range(2):
                both = [out[32 * i + PTS * c : 32 * i + PTS * c + PTS] for c in range(2)]
                for t in range(both[0].shape[1] // 128):
                    pieces = swap_halves(*[v[:, 128 * t : 128 * t + 128] for v in both])
                    for h in range(2):
                        o[2 * n + h, m + 2 * i, t // count, t % count] = pieces[h]


def early(chunk, z, parts, w0, w1, flops, steps=2):
    count = chunk[1]
    n = 8 // steps
    return pl.pallas_call(
        early_kernel,
        grid_spec=pltpu.PrefetchScalarGridSpec(
            num_scalar_prefetch=1,
            grid=(steps,),
            in_specs=[pl.BlockSpec((3, 2 * PTS, 128 * count * n), lambda d, zr: (0, 0, d))] * Q
            + [
                pl.BlockSpec((2, 64, 192), lambda d, zr: (0, 0, 0)),
                pl.BlockSpec((2, 2, 64, 192), lambda d, zr: (0, 0, 0, 0)),
            ],
            out_specs=pl.BlockSpec((Q, Q, n, count, PTS, 128), lambda d, zr: (0, 0, d, 0, 0, 0)),
            scratch_shapes=[pltpu.VMEM((Q, 3, 2 * PTS, 128 * count * n), jnp.float32)],
        ),
        out_shape=jax.ShapeDtypeStruct((Q, Q, 8, count, PTS, 128), jnp.float32),
        compiler_params=pltpu.CompilerParams(vmem_limit_bytes=VMEM),
        cost_estimate=cost(flops),
        name="early",
    )(z, *parts, w0, w1)


def late_kernel(yr, x, a0, a1, a2, a3, w2, w3, o0, o1, o2, o3, turns, done):
    y = yr[0]
    pairs, count = x.shape[2] // 2, x.shape[3]
    for e, a in enumerate((a0, a1, a2, a3)):
        turns[(y + Q - e) % Q] = a[...]
    for j in range(count):
        for t in range(Q):
            here = slice(PTS * t, PTS * t + PTS)
            angles = [jnp.concatenate([turns[e, j, l, here] for e in range(Q)], axis=0) for l in range(2)]
            split = [[swap_halves(x[e, t, 2 * g, j], x[e, t, 2 * g + 1, j]) for g in range(pairs)] for e in range(Q)]
            pair = [
                jnp.concatenate([jnp.concatenate([v[c] for v in row], axis=1) for row in split], axis=0)
                for c in range(2)
            ]
            for l, w in enumerate((w2, w3)):
                pair = [mm(w[t], v) for v in turn(*pair, angles[l])]
            for e in range(Q):
                for c in range(2):
                    done[e, j, c, here] = pair[c][PTS * e : PTS * e + PTS]
    for e, o in enumerate((o0, o1, o2, o3)):
        o[...] = done[(y + e) % Q]


def late(chunk, y, x, angles, w2, w3, flops, steps=2):
    tile, count = chunk
    n = 8 // steps
    return pl.pallas_call(
        late_kernel,
        grid_spec=pltpu.PrefetchScalarGridSpec(
            num_scalar_prefetch=1,
            grid=(steps,),
            in_specs=[pl.BlockSpec((Q, Q, n, count, PTS, 128), lambda d, yr: (0, 0, d, 0, 0, 0))]
            + [pl.BlockSpec((count, 2, Q * PTS, 64 * n), lambda d, yr: (tile // count, 0, 0, d))] * Q
            + [pl.BlockSpec((Q, 64, 192), lambda d, yr: (0, 0, 0))] * 2,
            out_specs=[pl.BlockSpec((count, 2, Q * PTS, 64 * n), lambda d, yr: (0, 0, 0, d))] * Q,
            scratch_shapes=[pltpu.VMEM((Q, count, 2, Q * PTS, 64 * n), jnp.float32)] * 2,
        ),
        out_shape=[jax.ShapeDtypeStruct((count, 2, Q * PTS, 512), jnp.float32)] * Q,
        compiler_params=pltpu.CompilerParams(vmem_limit_bytes=VMEM),
        cost_estimate=cost(flops),
        name="late",
    )(y, x, *angles, w2, w3)


def last_kernel(chunk, yr, *refs):
    tile, count = chunk
    ins, (o, room, ready, sems) = refs[:Q], refs[-4:]
    copies = []
    for g in range(4):
        here = slice(128 * g, 128 * g + 128)
        for j in range(count):
            for c in range(2):
                for e in range(Q):
                    at = (yr[0] + Q - e) % Q
                    for t in range(Q):
                        room[at % 2, 2 * t + at // 2] = ins[e][j, c, PTS * t : PTS * t + PTS, here]
                for i, v in enumerate(swap_halves(room[0], room[1])):
                    lanes = 128 * (count * (2 * g + i) + j)
                    ready[c, :, lanes : lanes + 128] = jnp.swapaxes(v, 0, 1).reshape(PTS * BOX, 128)
        for d in (2 * g, 2 * g + 1):
            copies.append(
                pltpu.make_async_copy(
                    ready.at[:, :, pl.ds(128 * count * d, 128 * count)],
                    o.at[:, :, pl.ds(512 * d + 128 * tile, 128 * count)],
                    sems.at[d],
                )
            )
            copies[-1].start()
    for copy in copies:
        copy.wait()


def last(chunk, y, parts, before, flops=1000):
    extra = [] if before is None else [before]
    count = chunk[1]
    return pl.pallas_call(
        functools.partial(last_kernel, chunk),
        grid_spec=pltpu.PrefetchScalarGridSpec(
            num_scalar_prefetch=1,
            grid=(1,),
            in_specs=[pl.BlockSpec((count, 2, Q * PTS, 512), lambda d, yr: (0, 0, 0, 0))] * Q
            + [pl.BlockSpec(memory_space=pl.ANY)] * len(extra),
            out_specs=pl.BlockSpec(memory_space=pl.ANY),
            scratch_shapes=[
                pltpu.VMEM((2, BOX, PTS, 128), jnp.float32),
                pltpu.VMEM((2, PTS * BOX, 1024 * count), jnp.float32),
                pltpu.SemaphoreType.DMA((8,)),
            ],
        ),
        out_shape=jax.ShapeDtypeStruct((2, PTS * BOX, FL), jnp.float32),
        input_output_aliases={Q + 1: 0} if extra else {},
        compiler_params=pltpu.CompilerParams(vmem_limit_bytes=VMEM),
        cost_estimate=cost(flops),
        name="last",
    )(y, *parts, *extra)


def pick(onehot, options):
    shape = onehot.shape + options.shape[1:]
    mask = onehot.reshape(onehot.shape + (1,) * (options.ndim - 1))
    return jnp.sum(jnp.where(mask, jnp.broadcast_to(options, shape), 0.0), axis=onehot.ndim - 1)


def halves(tables, classes, half):
    chosen = pick(classes[..., None] == jnp.arange(NCLASS), tables)
    upper = (half == 1)[:, None, None, None]
    own, other = chosen[:, :, 0, 0], chosen[:, :, 0, 1]
    own = jnp.where(upper, chosen[:, :, 1, 1], own)
    other = jnp.where(upper, chosen[:, :, 1, 0], other)
    return own, other


def two_parts(w):
    hi = lax.reduce_precision(w, 8, 7)
    lo = w - hi
    return jnp.concatenate([hi, hi, lo], axis=-1).astype(jnp.bfloat16)


def weights(cheb_tables, switch_kernel, box_class, y, z):
    near = jnp.arange(Q)
    byplace = box_class.reshape(4, Q, Q, BOX)
    mine_y = lax.dynamic_index_in_dim(byplace, y, 1, False)
    mine_z = lax.dynamic_index_in_dim(byplace, z, 2, False)
    mine_y = lax.dynamic_slice_in_dim(mine_y, 2 * z, 2, 2)
    mine_z = lax.dynamic_index_in_dim(mine_z.reshape(4, Q, Q, 2), y // 2, 3, False)
    by_z, by_y = mine_y.transpose(1, 0, 2), mine_z.transpose(1, 0, 2)
    eye = jnp.eye(2, dtype=jnp.float32)
    k0, k1 = switch_kernel[0], switch_kernel[1]
    kc = jnp.stack([jnp.stack([k0, -k1]), jnp.stack([k1, k0])])

    own, other = halves(cheb_tables[0], by_z[:, 0], near & 1)
    own, other = (v.reshape(2, 2, 2, PTS, PTS) for v in (own, other))
    w0 = jnp.einsum("qints,ij,nm->qintjms", own, eye, eye, precision=HIGHEST)
    w0 += jnp.einsum("qints,ij,nm->qintjms", other, 1 - eye, eye, precision=HIGHEST)
    w0 = w0.reshape(2, 64, 64)

    own, other = halves(cheb_tables[1], by_z[:, 1], (near >> 1) & 1)
    own, other = (
        jnp.einsum("cdtu,pus->pctds", kc, v.reshape(8, PTS, PTS), precision=HIGHEST).reshape(2, 2, 2, 2, PTS, 2, PTS)
        for v in (own, other)
    )
    w1 = jnp.einsum("imnctds,ih->nmicthds", own, eye, precision=HIGHEST)
    w1 += jnp.einsum("imnctds,ih->nmicthds", other, 1 - eye, precision=HIGHEST)
    w1 = w1.reshape(2, 2, 64, 64)

    late_w = []
    for l in (2, 3):
        own, other = halves(cheb_tables[l], by_y[:, l], (near >> (l - 2)) & 1)
        same = jnp.eye(Q, dtype=jnp.float32)
        swap = (near[:, None] ^ (l - 1) == near).astype(jnp.float32)
        w = jnp.einsum("ekts,eh->keths", own, same, precision=HIGHEST)
        w += jnp.einsum("ekts,eh->keths", other, swap, precision=HIGHEST)
        late_w.append(two_parts(w.reshape(Q, 64, 64)))
    return two_parts(w0), two_parts(w1), late_w[0], late_w[1]


def swapped(part, e, stride):
    count = lax.axis_size("space")

    def target(i):
        at = i // stride % Q
        return i + ((at + e) % Q - at) * stride

    return lax.ppermute(part, "space", [(i, target(i)) for i in range(count)])


def exchange(parts, stride):
    return [parts[0]] + [swapped(parts[e], e, stride) for e in range(1, Q)]


CHUNKS = ((0, 2), (2, 1), (3, 1))
LONG = 40_000_000_000


def on_device(source, angles, cheb_tables, switch_kernel, box_class):
    place = lax.axis_index("space")
    y, z = place // Q, place % Q
    yr, zr = y.reshape(1).astype(jnp.int32), z.reshape(1).astype(jnp.int32)
    source = source.reshape(2, PTS * BOX, FL)
    angles = angles.reshape(4, PTS * BOX, FL)
    tie = lax.optimization_barrier
    count = len(CHUNKS)

    sent, here, mixed, moved, back = [None] * count, [None] * count, [None] * count, [None] * count, [None] * count
    ready = first(CHUNKS[0], zr, source, angles)
    ready, source, angles = tie((ready, source, angles))
    here[0] = exchange(ready, 1)
    turns = share(yr, angles)
    turns, source, angles = tie((turns, source, angles))
    turns = list(turns)
    turns[1], turns[3] = swapped(turns[1], 1, Q), swapped(turns[3], 3, Q)
    for k in range(1, count):
        sent[k] = first(CHUNKS[k], zr, source, angles)
    sent[1:], cheb_tables, switch_kernel, box_class = tie((sent[1:], cheb_tables, switch_kernel, box_class))
    w0, w1, w2, w3 = weights(cheb_tables, switch_kernel, box_class, y, z)
    here[0], sent[1:], w0, w1, w2, w3 = tie((here[0], sent[1:], w0, w1, w2, w3))

    result = [None]

    def do_late(k):
        if k:
            if k + 1 == len(CHUNKS):
                result[0] = last(CHUNKS[0], yr, back[0], None, 10_000_000_000)
                result[0], back[k - 1][1], moved[k] = tie((result[0], back[k - 1][1], moved[k]))
        done = late(CHUNKS[k], yr, moved[k], turns, w2, w3, (8_000_000_000, 1000, 1000)[k])
        back[k] = exchange(done, Q)

    for k, chunk in enumerate(CHUNKS):
        if k + 1 < count:
            here[k], sent[k + 1] = tie((here[k], sent[k + 1]))
            here[k + 1] = exchange(sent[k + 1], 1)
        if k == 1:
            here[k], turns[2] = tie((here[k], turns[2]))
        mixed[k] = early(chunk, zr, here[k], w0, w1, (1000, LONG, 3_000_000_000)[k])
        if k:
            moved[k - 1], mixed[k] = tie((moved[k - 1], mixed[k]))
        if k == 0:
            turns[1], turns[2], turns[3] = tie((turns[1], turns[2], turns[3]))
            turns[2] = swapped(turns[2], 2, Q)
        all_parts = lax.all_to_all(mixed[k].reshape(128, chunk[1], PTS, 128), ("space", "freq"), 0, 0, tiled=True)
        moved[k] = all_parts.reshape(Q, Q, 8, chunk[1], PTS, 128)
        if k:
            do_late(k - 1)
            if k + 1 < count:
                back[k - 1][0], here[k + 1] = tie((back[k - 1][0], here[k + 1]))
    do_late(count - 1)
    for k in range(1, count):
        if k + 1 < count:
            back[k], back[k + 1][0] = tie((back[k], back[k + 1][0]))
        result[0] = last(CHUNKS[k], yr, back[k], result[0])
    return result[0].reshape(2, PTS, BOX, FL)


def solution(mesh):
    in_specs = (P(None, None, "space", "freq"), P(None, None, "space", "freq"), P(), P(), P())
    out_specs = P(None, None, "space", "freq")
    return jax.shard_map(
        on_device, mesh=mesh, in_specs=in_specs, out_specs=out_specs, check_vma=False
    )
```

```python
import functools

import jax
import jax.numpy as jnp
from jax import lax
from jax.experimental import pallas as pl
from jax.experimental.pallas import tpu as pltpu
from jax.sharding import PartitionSpec as P

NCLASS = 4
PTS = 16
BOX = 8
FL = 4096
Q = 4
HIGHEST = lax.Precision.HIGHEST
SIN = (1.0, -0.04166664555668831, 0.0005208156653679907, -3.095163492616848e-06, 1.0176427700514523e-08)
COS = (0.9999999403953552, -0.1249997615814209, 0.002603973727673292, -2.1646354070981033e-05, 9.044205739883182e-08)
VMEM = 56 * 1024 * 1024


def cost(flops=1000):
    return pl.CostEstimate(flops=flops, bytes_accessed=1000, transcendentals=0)


def poly(coefs, u):
    r = coefs[-1]
    for c in coefs[-2::-1]:
        r = r * u + c
    return r


def turn(re, im, a):
    u = a * a
    s2 = a * poly(SIN, u)
    sine = s2 * poly(COS, u)
    cosine = 1.0 - 0.5 * (s2 * s2)
    return cosine * re - sine * im, sine * re + cosine * im


def split3(x):
    hi = x.astype(jnp.bfloat16)
    lo = (x - hi.astype(jnp.float32)).astype(jnp.bfloat16)
    return jnp.concatenate([hi, lo, hi], axis=0)


def mm(w, x):
    return jnp.dot(w, split3(x), preferred_element_type=jnp.float32)


def by_box(v):
    return jnp.swapaxes(v.reshape(PTS, BOX, v.shape[-1]), 0, 1)


def swap_halves(a, b):
    low = lax.broadcasted_iota(jnp.int32, a.shape, a.ndim - 1) < 64
    return (
        jnp.where(low, a, pltpu.roll(b, 64, a.ndim - 1)),
        jnp.where(low, pltpu.roll(a, 64, a.ndim - 1), b),
    )


def first_kernel(n, zr, *refs):
    src, ang, outs, room = refs[:n], refs[n : 2 * n], refs[2 * n : 2 * n + Q], refs[-1]
    lanes = room.shape[-1]
    for d in range(n):
        re, im = turn(src[d][0], src[d][1], ang[d][0])
        for c, v in enumerate((re, im, ang[d][1])):
            room[c] = by_box(v)
        for e, o in enumerate(outs):
            for c in range(3):
                for i in range(2):
                    o[c, PTS * i : PTS * i + PTS, lanes * d : lanes * d + lanes] = room[c, 2 * ((zr[0] + e) % Q) + i]


def first(chunk, z, source, angles):
    tile, count = chunk
    lanes, n = 128 * count, 4

    def spec(d):
        return pl.BlockSpec((2, PTS * BOX, lanes), lambda g, zr: (0, 0, (n * g + d) * (4 // count) + tile // count))

    return pl.pallas_call(
        functools.partial(first_kernel, n),
        grid_spec=pltpu.PrefetchScalarGridSpec(
            num_scalar_prefetch=1,
            grid=(8 // n,),
            in_specs=[spec(d) for d in range(n)] * 2,
            out_specs=[pl.BlockSpec((3, 2 * PTS, lanes * n), lambda g, zr: (0, 0, g))] * Q,
            scratch_shapes=[pltpu.VMEM((3, BOX, PTS, lanes), jnp.float32)],
        ),
        out_shape=[jax.ShapeDtypeStruct((3, 2 * PTS, lanes * 8), jnp.float32)] * Q,
        compiler_params=pltpu.CompilerParams(vmem_limit_bytes=VMEM),
        cost_estimate=cost(),
        name="first",
    )(z, *[source] * n, *[angles] * n)


def share_kernel(yr, a, o0, o1, o2, o3, room):
    for l in range(2):
        for g in range(2):
            for t in range(Q):
                pair = [
                    by_box(a[l, :, 512 * d + 128 * t : 512 * d + 128 * t + 128]).reshape(Q, 2, PTS, 128)
                    for d in (2 * g, 2 * g + 1)
                ]
                for n in range(2):
                    for h, v in enumerate(swap_halves(pair[0][:, n], pair[1][:, n])):
                        room[2 * n + h] = v.reshape(Q * PTS, 128)
                for e, o in enumerate((o0, o1, o2, o3)):
                    o[t, l, :, 128 * g : 128 * g + 128] = room[(yr[0] + e) % Q]


def share(y, angles):
    return pl.pallas_call(
        share_kernel,
        grid_spec=pltpu.PrefetchScalarGridSpec(
            num_scalar_prefetch=1,
            grid=(2,),
            in_specs=[pl.BlockSpec((2, PTS * BOX, 2048), lambda d, yr: (1, 0, d))],
            out_specs=[pl.BlockSpec((4, 2, Q * PTS, 256), lambda d, yr: (0, 0, 0, d))] * Q,
            scratch_shapes=[pltpu.VMEM((Q, Q * PTS, 128), jnp.float32)],
        ),
        out_shape=[jax.ShapeDtypeStruct((4, 2, Q * PTS, 512), jnp.float32)] * Q,
        compiler_params=pltpu.CompilerParams(vmem_limit_bytes=VMEM),
        cost_estimate=cost(),
        name="share",
    )(y, angles)


def early_kernel(zr, r0, r1, r2, r3, w0, w1, o, r):
    for e, v in enumerate((r0, r1, r2, r3)):
        r[(zr[0] + Q - e) % Q] = v[...]
    count = o.shape[3]
    x = []
    for q in range(2):
        part = []
        for c in range(2):
            rows = jnp.concatenate([r[2 * q + i, c] for i in range(2)], axis=0)
            part.append(mm(w0[q], rows))
        angle = jnp.concatenate([r[2 * q + i, 2] for i in range(2)], axis=0)
        x.append(turn(*part, angle))
    for n in range(2):
        for m in range(2):
            here = slice(32 * m + PTS * n, 32 * m + PTS * n + PTS)
            rows = jnp.concatenate([x[i][c][here] for i in range(2) for c in range(2)], axis=0)
            out = mm(w1[n, m], rows)
            for i in range(2):
                both = [out[32 * i + PTS * c : 32 * i + PTS * c + PTS] for c in range(2)]
                for t in range(both[0].shape[1] // 128):
                    pieces = swap_halves(*[v[:, 128 * t : 128 * t + 128] for v in both])
                    for h in range(2):
                        o[2 * n + h, m + 2 * i, t // count, t % count] = pieces[h]


def early(chunk, z, parts, w0, w1, flops, steps=2):
    count = chunk[1]
    n = 8 // steps
    return pl.pallas_call(
        early_kernel,
        grid_spec=pltpu.PrefetchScalarGridSpec(
            num_scalar_prefetch=1,
            grid=(steps,),
            in_specs=[pl.BlockSpec((3, 2 * PTS, 128 * count * n), lambda d, zr: (0, 0, d))] * Q
            + [
                pl.BlockSpec((2, 64, 192), lambda d, zr: (0, 0, 0)),
                pl.BlockSpec((2, 2, 64, 192), lambda d, zr: (0, 0, 0, 0)),
            ],
            out_specs=pl.BlockSpec((Q, Q, n, count, PTS, 128), lambda d, zr: (0, 0, d, 0, 0, 0)),
            scratch_shapes=[pltpu.VMEM((Q, 3, 2 * PTS, 128 * count * n), jnp.float32)],
        ),
        out_shape=jax.ShapeDtypeStruct((Q, Q, 8, count, PTS, 128), jnp.float32),
        compiler_params=pltpu.CompilerParams(vmem_limit_bytes=VMEM),
        cost_estimate=cost(flops),
        name="early",
    )(z, *parts, w0, w1)


def late_kernel(yr, x, a0, a1, a2, a3, w2, w3, o0, o1, o2, o3, turns, done):
    y = yr[0]
    pairs, count = x.shape[2] // 2, x.shape[3]
    for e, a in enumerate((a0, a1, a2, a3)):
        turns[(y + Q - e) % Q] = a[...]
    for j in range(count):
        for t in range(Q):
            here = slice(PTS * t, PTS * t + PTS)
            angles = [jnp.concatenate([turns[e, j, l, here] for e in range(Q)], axis=0) for l in range(2)]
            split = [[swap_halves(x[e, t, 2 * g, j], x[e, t, 2 * g + 1, j]) for g in range(pairs)] for e in range(Q)]
            pair = [
                jnp.concatenate([jnp.concatenate([v[c] for v in row], axis=1) for row in split], axis=0)
                for c in range(2)
            ]
            for l, w in enumerate((w2, w3)):
                pair = [mm(w[t], v) for v in turn(*pair, angles[l])]
            for e in range(Q):
                for c in range(2):
                    done[e, j, c, here] = pair[c][PTS * e : PTS * e + PTS]
    for e, o in enumerate((o0, o1, o2, o3)):
        o[...] = done[(y + e) % Q]


def late(chunk, y, x, angles, w2, w3, flops, steps=2):
    tile, count = chunk
    n = 8 // steps
    return pl.pallas_call(
        late_kernel,
        grid_spec=pltpu.PrefetchScalarGridSpec(
            num_scalar_prefetch=1,
            grid=(steps,),
            in_specs=[pl.BlockSpec((Q, Q, n, count, PTS, 128), lambda d, yr: (0, 0, d, 0, 0, 0))]
            + [pl.BlockSpec((count, 2, Q * PTS, 64 * n), lambda d, yr: (tile // count, 0, 0, d))] * Q
            + [pl.BlockSpec((Q, 64, 192), lambda d, yr: (0, 0, 0))] * 2,
            out_specs=[pl.BlockSpec((count, 2, Q * PTS, 64 * n), lambda d, yr: (0, 0, 0, d))] * Q,
            scratch_shapes=[pltpu.VMEM((Q, count, 2, Q * PTS, 64 * n), jnp.float32)] * 2,
        ),
        out_shape=[jax.ShapeDtypeStruct((count, 2, Q * PTS, 512), jnp.float32)] * Q,
        compiler_params=pltpu.CompilerParams(vmem_limit_bytes=VMEM),
        cost_estimate=cost(flops),
        name="late",
    )(y, x, *angles, w2, w3)


def last_kernel(chunk, yr, *refs):
    tile, count = chunk
    ins, (o, room, ready, sems) = refs[:Q], refs[-4:]
    copies = []
    for g in range(4):
        here = slice(128 * g, 128 * g + 128)
        for j in range(count):
            for c in range(2):
                for e in range(Q):
                    at = (yr[0] + Q - e) % Q
                    for t in range(Q):
                        room[at % 2, 2 * t + at // 2] = ins[e][j, c, PTS * t : PTS * t + PTS, here]
                for i, v in enumerate(swap_halves(room[0], room[1])):
                    lanes = 128 * (count * (2 * g + i) + j)
                    ready[c, :, lanes : lanes + 128] = jnp.swapaxes(v, 0, 1).reshape(PTS * BOX, 128)
        for d in (2 * g, 2 * g + 1):
            copies.append(
                pltpu.make_async_copy(
                    ready.at[:, :, pl.ds(128 * count * d, 128 * count)],
                    o.at[:, :, pl.ds(512 * d + 128 * tile, 128 * count)],
                    sems.at[d],
                )
            )
            copies[-1].start()
    for copy in copies:
        copy.wait()


def last(chunk, y, parts, before, flops=1000):
    extra = [] if before is None else [before]
    count = chunk[1]
    return pl.pallas_call(
        functools.partial(last_kernel, chunk),
        grid_spec=pltpu.PrefetchScalarGridSpec(
            num_scalar_prefetch=1,
            grid=(1,),
            in_specs=[pl.BlockSpec((count, 2, Q * PTS, 512), lambda d, yr: (0, 0, 0, 0))] * Q
            + [pl.BlockSpec(memory_space=pl.ANY)] * len(extra),
            out_specs=pl.BlockSpec(memory_space=pl.ANY),
            scratch_shapes=[
                pltpu.VMEM((2, BOX, PTS, 128), jnp.float32),
                pltpu.VMEM((2, PTS * BOX, 1024 * count), jnp.float32),
                pltpu.SemaphoreType.DMA((8,)),
            ],
        ),
        out_shape=jax.ShapeDtypeStruct((2, PTS * BOX, FL), jnp.float32),
        input_output_aliases={Q + 1: 0} if extra else {},
        compiler_params=pltpu.CompilerParams(vmem_limit_bytes=VMEM),
        cost_estimate=cost(flops),
        name="last",
    )(y, *parts, *extra)


def pick(onehot, options):
    shape = onehot.shape + options.shape[1:]
    mask = onehot.reshape(onehot.shape + (1,) * (options.ndim - 1))
    return jnp.sum(jnp.where(mask, jnp.broadcast_to(options, shape), 0.0), axis=onehot.ndim - 1)


def halves(tables, classes, half):
    chosen = pick(classes[..., None] == jnp.arange(NCLASS), tables)
    upper = (half == 1)[:, None, None, None]
    own, other = chosen[:, :, 0, 0], chosen[:, :, 0, 1]
    own = jnp.where(upper, chosen[:, :, 1, 1], own)
    other = jnp.where(upper, chosen[:, :, 1, 0], other)
    return own, other


def two_parts(w):
    hi = lax.reduce_precision(w, 8, 7)
    lo = w - hi
    return jnp.concatenate([hi, hi, lo], axis=-1).astype(jnp.bfloat16)


def weights(cheb_tables, switch_kernel, box_class, y, z):
    near = jnp.arange(Q)
    byplace = box_class.reshape(4, Q, Q, BOX)
    mine_y = lax.dynamic_index_in_dim(byplace, y, 1, False)
    mine_z = lax.dynamic_index_in_dim(byplace, z, 2, False)
    mine_y = lax.dynamic_slice_in_dim(mine_y, 2 * z, 2, 2)
    mine_z = lax.dynamic_index_in_dim(mine_z.reshape(4, Q, Q, 2), y // 2, 3, False)
    by_z, by_y = mine_y.transpose(1, 0, 2), mine_z.transpose(1, 0, 2)
    eye = jnp.eye(2, dtype=jnp.float32)
    k0, k1 = switch_kernel[0], switch_kernel[1]
    kc = jnp.stack([jnp.stack([k0, -k1]), jnp.stack([k1, k0])])

    own, other = halves(cheb_tables[0], by_z[:, 0], near & 1)
    own, other = (v.reshape(2, 2, 2, PTS, PTS) for v in (own, other))
    w0 = jnp.einsum("qints,ij,nm->qintjms", own, eye, eye, precision=HIGHEST)
    w0 += jnp.einsum("qints,ij,nm->qintjms", other, 1 - eye, eye, precision=HIGHEST)
    w0 = w0.reshape(2, 64, 64)

    own, other = halves(cheb_tables[1], by_z[:, 1], (near >> 1) & 1)
    own, other = (
        jnp.einsum("cdtu,pus->pctds", kc, v.reshape(8, PTS, PTS), precision=HIGHEST).reshape(2, 2, 2, 2, PTS, 2, PTS)
        for v in (own, other)
    )
    w1 = jnp.einsum("imnctds,ih->nmicthds", own, eye, precision=HIGHEST)
    w1 += jnp.einsum("imnctds,ih->nmicthds", other, 1 - eye, precision=HIGHEST)
    w1 = w1.reshape(2, 2, 64, 64)

    late_w = []
    for l in (2, 3):
        own, other = halves(cheb_tables[l], by_y[:, l], (near >> (l - 2)) & 1)
        same = jnp.eye(Q, dtype=jnp.float32)
        swap = (near[:, None] ^ (l - 1) == near).astype(jnp.float32)
        w = jnp.einsum("ekts,eh->keths", own, same, precision=HIGHEST)
        w += jnp.einsum("ekts,eh->keths", other, swap, precision=HIGHEST)
        late_w.append(two_parts(w.reshape(Q, 64, 64)))
    return two_parts(w0), two_parts(w1), late_w[0], late_w[1]


def swapped(part, e, stride):
    count = lax.axis_size("space")

    def target(i):
        at = i // stride % Q
        return i + ((at + e) % Q - at) * stride

    return lax.ppermute(part, "space", [(i, target(i)) for i in range(count)])


def exchange(parts, stride):
    return [parts[0]] + [swapped(parts[e], e, stride) for e in range(1, Q)]


CHUNKS = ((0, 2), (2, 1), (3, 1))
LONG = 40_000_000_000


def on_device(source, angles, cheb_tables, switch_kernel, box_class):
    place = lax.axis_index("space")
    y, z = place // Q, place % Q
    yr, zr = y.reshape(1).astype(jnp.int32), z.reshape(1).astype(jnp.int32)
    source = source.reshape(2, PTS * BOX, FL)
    angles = angles.reshape(4, PTS * BOX, FL)
    tie = lax.optimization_barrier
    count = len(CHUNKS)

    sent, here, mixed, moved, back = [None] * count, [None] * count, [None] * count, [None] * count, [None] * count
    ready = first(CHUNKS[0], zr, source, angles)
    ready, source, angles = tie((ready, source, angles))
    here[0] = exchange(ready, 1)
    turns = share(yr, angles)
    turns, source, angles = tie((turns, source, angles))
    turns = list(turns)
    turns[1], turns[3] = swapped(turns[1], 1, Q), swapped(turns[3], 3, Q)
    for k in range(1, count):
        sent[k] = first(CHUNKS[k], zr, source, angles)
    sent[1:], cheb_tables, switch_kernel, box_class = tie((sent[1:], cheb_tables, switch_kernel, box_class))
    w0, w1, w2, w3 = weights(cheb_tables, switch_kernel, box_class, y, z)
    here[0], sent[1:], w0, w1, w2, w3 = tie((here[0], sent[1:], w0, w1, w2, w3))

    result = [None]

    def do_late(k):
        if k:
            if k + 1 == len(CHUNKS):
                result[0] = last(CHUNKS[0], yr, back[0], None, 10_000_000_000)
                result[0], moved[k] = tie((result[0], moved[k]))
        done = late(CHUNKS[k], yr, moved[k], turns, w2, w3, (8_000_000_000, 1000, 1000)[k])
        back[k] = exchange(done, Q)

    for k, chunk in enumerate(CHUNKS):
        if k + 1 < count:
            here[k], sent[k + 1] = tie((here[k], sent[k + 1]))
            here[k + 1] = exchange(sent[k + 1], 1)
        if k == 1:
            here[k], turns[2] = tie((here[k], turns[2]))
        mixed[k] = early(chunk, zr, here[k], w0, w1, (1000, LONG, 3_000_000_000)[k])
        if k:
            moved[k - 1], mixed[k] = tie((moved[k - 1], mixed[k]))
        if k == 0:
            turns[1], turns[2], turns[3] = tie((turns[1], turns[2], turns[3]))
            turns[2] = swapped(turns[2], 2, Q)
        all_parts = lax.all_to_all(mixed[k].reshape(128, chunk[1], PTS, 128), ("space", "freq"), 0, 0, tiled=True)
        moved[k] = all_parts.reshape(Q, Q, 8, chunk[1], PTS, 128)
        if k:
            do_late(k - 1)
            if k + 1 < count:
                back[k - 1][0], here[k + 1] = tie((back[k - 1][0], here[k + 1]))
    do_late(count - 1)
    for k in range(1, count):
        if k + 1 < count:
            back[k], back[k + 1][0] = tie((back[k], back[k + 1][0]))
        result[0] = last(CHUNKS[k], yr, back[k], result[0], 5_000_000_000 if k == 1 else 1000)
    return result[0].reshape(2, PTS, BOX, FL)


def solution(mesh):
    in_specs = (P(None, None, "space", "freq"), P(None, None, "space", "freq"), P(), P(), P())
    out_specs = P(None, None, "space", "freq")
    return jax.shard_map(
        on_device, mesh=mesh, in_specs=in_specs, out_specs=out_specs, check_vma=False
    )
```
